256 devices in a mesh: sub: 128 (over z, y, x), col: 2 (over core).
Axes of the slice: x: 4, y: 4, z: 8, core: 2. Of those that a mesh axis runs over, the one named last changes fastest.
Arguments:
- prolong: bfloat16 [524288, 256], P('sub', 'col'), may hold values from -2.390625 to 2.390625
- tiles: bfloat16 [128, 5, 96, 128, 128], P('sub', None, 'col'), may hold values from -0.046875 to 0.046875
- tile_rows: int32 [128, 5, 96], P('sub', None, 'col'), may hold values from 0 to 31
- tile_cols: int32 [128, 5, 96], P('sub', None, 'col'), may hold values from 0 to 31
- counts: int32 [128, 5], P('sub'), may hold values from 32 to 96
Outputs:
- coarse_upper: float32 [128, 5, 256, 256], P('sub', None, 'col')
- coarse_lower: float32 [128, 4, 256, 256], P('sub', None, None, 'col')
The draws below stay inside these ranges and needn't reach their ends.
Inputs may be any that keep to these rules, and one draw needn't show every extreme that they name: Slots at and beyond counts are ignored; counts reach 96 for some subdomain and offset.
All inputs are finite; a program needn't handle non-finite values.
Results may differ from the reference program's by a relative error of at most 0.0029.
Values may be sent and summed in bfloat16 or wider, within the bound.
No kernel may reach another device: no remote copies, remote signals or barrier semaphores. Data moves between devices by JAX's collectives and lax.ppermute only.
A program may use at most 128 MiB of HBM per device.

```python
import jax
import jax.numpy as jnp
from jax import lax

TILE = 128
FR = 4096
CB = 256
OFF = 4
MAXP = 96
NSUB = 128
NFINE = 524288


def place_ends(entries, key, least, top_value):
    extent = entries.shape
    index_at = [jax.random.randint(jax.random.fold_in(key, axis), (), 0, extent[axis]) for axis in range(len(extent))]
    entries = entries.at[tuple(index_at)].set(least)
    longest = extent.index(max(extent))
    index_at[longest] = (index_at[longest] + 1) % extent[longest]
    return entries.at[tuple(index_at)].set(top_value)


def level_of(key, extent, cuts, low, largest):
    loudness = 1.0
    for axis_at, parts in cuts:
        heights = jax.random.uniform(jax.random.fold_in(jax.random.fold_in(key, 6), axis_at), (parts,), jnp.float32, low / len(cuts), largest / len(cuts))
        loudness = loudness * jnp.repeat(jnp.exp(heights), extent[axis_at] // parts).reshape((-1,) + (1,) * (len(extent) - 1 - axis_at))
    return loudness


def gaussian(stream_key, shape, spread, reach, cuts=(), kind=jnp.bfloat16):
    drawn = jax.random.normal(stream_key, shape, jnp.float32) * spread
    if len(cuts) > 0:
        drawn = level_of(stream_key, shape, cuts, -0.22, 0.18) * drawn
    return jnp.clip(drawn, min=-reach, max=reach).astype(kind)


def setup_inputs(seed: int = 0) -> dict:
    keys = jax.random.split(jax.random.key(seed), 6)
    return {
        "prolong": gaussian(keys[0], (NFINE, CB), 0.4, 2.390625, ((0, 128), (1, 2))),
        "tiles": gaussian(keys[1], (NSUB, OFF + 1, MAXP, TILE, TILE), (TILE * TILE) ** -0.5, 0.046875, ((0, 128), (2, 2))),
        "tile_rows": place_ends(jax.random.randint(keys[2], (NSUB, OFF + 1, MAXP), 0, FR // TILE), jax.random.fold_in(keys[2], 1), 0, (FR // TILE) - 1).astype(jnp.int32),
        "tile_cols": place_ends(jax.random.randint(keys[3], (NSUB, OFF + 1, MAXP), 0, FR // TILE), jax.random.fold_in(keys[3], 1), 0, (FR // TILE) - 1).astype(jnp.int32),
        "counts": place_ends(jax.random.randint(keys[4], (NSUB, OFF + 1), MAXP // 3, MAXP + 1), jax.random.fold_in(keys[4], 1), MAXP // 3, MAXP).astype(jnp.int32),
    }


def reference(prolong, tiles, tile_rows, tile_cols, counts):
    padded = jnp.concatenate([prolong, jnp.zeros((OFF * FR, CB), prolong.dtype)], 0)

    def one_sub(index):
        own = lax.dynamic_slice_in_dim(padded, index * FR, FR, 0).reshape(FR // TILE, TILE, CB)
        blocks = []
        for offset in range(OFF + 1):
            far = lax.dynamic_slice_in_dim(padded, (index + offset) * FR, FR, 0).reshape(FR // TILE, TILE, CB)
            a_tiles = tiles[index, offset].astype(jnp.float32)
            rows_idx = tile_rows[index, offset]
            cols_idx = tile_cols[index, offset]
            live = (jnp.arange(MAXP, dtype=jnp.int32) < counts[index, offset]).astype(jnp.float32)
            applied = jnp.einsum("pkl,plc->pkc", a_tiles, far[cols_idx].astype(jnp.float32))
            applied = (applied * live[:, None, None]).astype(jnp.bfloat16)
            applied = lax.optimization_barrier(applied).astype(jnp.float32)
            blocks.append(jnp.einsum("pkr,pkc->rc", own[rows_idx].astype(jnp.float32), applied))
        return jnp.stack(blocks)

    coarse_upper = lax.map(one_sub, jnp.arange(NSUB, dtype=jnp.int32))
    lowers = []
    for offset in range(1, OFF + 1):
        moved = jnp.concatenate([jnp.zeros((offset, CB, CB), jnp.float32), coarse_upper[:NSUB - offset, offset]], 0)
        lowers.append(jnp.swapaxes(moved, 1, 2))
    coarse_lower = jnp.stack(lowers, 1)
    return coarse_upper, coarse_lower
```

```python
import functools

import jax
import jax.numpy as jnp
from jax import lax
from jax.experimental import pallas as pl
from jax.experimental.pallas import tpu as pltpu
from jax.sharding import PartitionSpec as P

NSUB = 128
ROW = 4
GROUP = 4


def shift(value, distance):
    route = [((s + distance) % NSUB, s) for s in range(NSUB)]
    return lax.ppermute(value, "sub", route)


def swap(value):
    return lax.ppermute(value, "col", [(0, 1), (1, 0)])


def weights_kernel(rows, cols, live, p0, p1, tiles, out, pt, acc):
    o = pl.program_id(0)
    nt = acc.shape[0]
    edge = tiles.shape[-1]

    @pl.when(o == 0)
    def _():
        for t in range(nt):
            pt[t, :edge, :] = p0[t * edge : (t + 1) * edge, :].T
            pt[t, edge:, :] = p1[t * edge : (t + 1) * edge, :].T

    acc[...] = jnp.zeros_like(acc)
    n = live[o]

    def group(g, carry):
        parts = []
        for j in range(GROUP):
            p = g * GROUP + j
            part = jnp.dot(pt[rows[o, p]], tiles[0, p], preferred_element_type=jnp.float32)
            parts.append(jnp.where(p < n, part, 0.0))
        for j in range(GROUP):
            c = cols[o, g * GROUP + j]
            acc[c] += parts[j]
        return carry

    lax.fori_loop(0, (n + GROUP - 1) // GROUP, group, 0)
    for t in range(nt):
        out[0, :, t * edge : (t + 1) * edge] = acc[t].astype(out.dtype)


def weights(rows, cols, live, p0, p1, tiles):
    offsets, slots, edge, _ = tiles.shape
    fine = p0.shape[0]
    nt = fine // edge
    whole = lambda o, *_: (0, 0)
    return pl.pallas_call(
        weights_kernel,
        grid_spec=pltpu.PrefetchScalarGridSpec(
            num_scalar_prefetch=3,
            grid=(offsets,),
            in_specs=[
                pl.BlockSpec((fine, edge), whole),
                pl.BlockSpec((fine, edge), whole),
                pl.BlockSpec((1, slots, edge, edge), lambda o, *_: (o, 0, 0, 0)),
            ],
            out_specs=pl.BlockSpec((1, 2 * edge, fine), lambda o, *_: (o, 0, 0)),
            scratch_shapes=[
                pltpu.VMEM((nt, 2 * edge, edge), jnp.bfloat16),
                pltpu.VMEM((nt, 2 * edge, edge), jnp.float32),
            ],
        ),
        out_shape=jax.ShapeDtypeStruct((offsets, 2 * edge, fine), jnp.bfloat16),
        compiler_params=pltpu.CompilerParams(vmem_limit_bytes=32 * 1024 * 1024),
        cost_estimate=pl.CostEstimate(
            flops=offsets * slots * 4 * edge**3, bytes_accessed=20 * 2**20, transcendentals=0
        ),
    )(rows, cols, live, p0, p1, tiles)


def on_device(prolong, tiles, tile_rows, tile_cols, counts):
    slots = tiles.shape[2]
    offsets = tiles.shape[1]
    fine = prolong.shape[0]
    half = fine // 2
    core = lax.axis_index("col")
    sub = lax.axis_index("sub")
    pa, pb = prolong[:half], prolong[half:]

    away = [(s, (s - 1) % NSUB) for s in range(NSUB) if s % ROW != 0]
    wrap = [(s, s + ROW - 1) for s in range(NSUB) if s % ROW == 0]
    y_a = shift(pa, 4)
    a_a = lax.ppermute(pa, "sub", away)
    y_b = shift(pb, 4)
    a_b = lax.ppermute(pb, "sub", away)
    a_a = a_a + lax.ppermute(y_a, "sub", wrap)
    a_b = a_b + lax.ppermute(y_b, "sub", wrap)
    b_a = shift(y_a, -1)
    b_b = shift(y_b, -1)
    d_a = shift(a_a, 1)
    d_b = shift(b_b, -1)
    panels = [(pa, pb), (a_a, a_b), (d_a, d_b), (b_a, b_b), (y_a, y_b)]

    other = swap(prolong)
    first = jnp.where(core == 0, prolong, other)
    second = jnp.where(core == 0, other, prolong)
    live = jnp.clip(counts[0] - core * slots, 0, slots)
    live = jnp.where(sub + jnp.arange(offsets) < NSUB, live, 0).astype(jnp.int32)
    mine = weights(tile_rows[0], tile_cols[0], live, first, second, tiles[0])
    theirs = swap(mine)

    def dot(w, p):
        return jnp.dot(w, p, preferred_element_type=jnp.float32)

    uppers = []
    lowers = []
    width = prolong.shape[1]
    for o in range(offsets):
        a, b = panels[o]
        c = (dot(mine[o, :, :half], a) + dot(theirs[o, :, :half], a)) + (
            dot(mine[o, :, half:], b) + dot(theirs[o, :, half:], b)
        )
        keep = jnp.where(core == 0, c[:width], c[width:])
        give = jnp.where(core == 0, c[width:], c[:width])
        got = swap(give)
        upper = jnp.concatenate(
            [jnp.where(core == 0, keep, got), jnp.where(core == 0, got, keep)], axis=1
        )
        uppers.append(upper)
        if o > 0:
            arrived = lax.ppermute(upper, "sub", [(s, s + o) for s in range(NSUB - o)])
            lowers.append(arrived.T)
    return jnp.stack(uppers)[None], jnp.stack(lowers)[None]


def solution(mesh):
    placed = (
        P("sub", "col"),
        P("sub", None, "col", None, None),
        P("sub", None, "col"),
        P("sub", None, "col"),
        P("sub", None),
    )
    return jax.shard_map(
        on_device,
        mesh=mesh,
        in_specs=placed,
        out_specs=(P("sub", None, "col", None), P("sub", None, None, "col")),
        check_vma=False,
    )
```

```python
import jax
import jax.numpy as jnp
from jax import lax
from jax.experimental import pallas as pl
from jax.experimental.pallas import tpu as pltpu
from jax.sharding import PartitionSpec as P

NSUB = 128
ROW = 4
GROUP = 16
CHUNK = 2048
VMEM = 24 * 2**20


def shift(value, distance):
    route = [((s + distance) % NSUB, s) for s in range(NSUB)]
    return lax.ppermute(value, "sub", route)


def swap(value):
    return lax.ppermute(value, "col", [(0, 1), (1, 0)])


def weights_kernel(rows, cols, live, core, p0, p1, tiles, out, pt, acc, seen):
    o = pl.program_id(0)
    edge = tiles.shape[-1]
    nt = p0.shape[0] // edge

    @pl.when(o == 0)
    def _():
        for t in range(nt):
            seen[t] = 0
        seen[nt] = 0

    for at, half in enumerate((p0, p1)):

        @pl.when((o == 0) & (core[0] == 0))
        def _():
            for t in range(nt):
                pt[t, at * edge : (at + 1) * edge, :] = half[t * edge : (t + 1) * edge, :].T

        @pl.when((o == 0) & (core[0] == 1))
        def _():
            for t in range(nt):
                pt[t, (1 - at) * edge : (2 - at) * edge, :] = half[t * edge : (t + 1) * edge, :].T

    n = live[o]

    def group(g, carry):
        parts = []
        for j in range(GROUP):
            p = g * GROUP + j
            parts.append(
                jnp.dot(pt[rows[o, p]], tiles[0, p], preferred_element_type=jnp.float32)
            )
        for j in range(GROUP):
            p = g * GROUP + j
            c = jnp.where(p < n, cols[o, p], nt)
            fresh = seen[c] != o + 1
            seen[c] = o + 1
            acc[c] = jnp.where(fresh, parts[j], acc[c] + parts[j])
        return carry

    lax.fori_loop(0, (n + GROUP - 1) // GROUP, group, 0)
    for t in range(nt):
        out[0, :, t * edge : (t + 1) * edge] = jnp.where(seen[t] == o + 1, acc[t], 0.0).astype(
            out.dtype
        )


def weights(rows, cols, live, core, p0, p1, tiles):
    offsets, slots, edge, _ = tiles.shape
    fine = p0.shape[0]
    nt = fine // edge
    whole = lambda o, *_: (0, 0)
    return pl.pallas_call(
        weights_kernel,
        grid_spec=pltpu.PrefetchScalarGridSpec(
            num_scalar_prefetch=4,
            grid=(offsets,),
            in_specs=[
                pl.BlockSpec((fine, edge), whole),
                pl.BlockSpec((fine, edge), whole),
                pl.BlockSpec((1, slots, edge, edge), lambda o, *_: (o, 0, 0, 0)),
            ],
            out_specs=pl.BlockSpec((1, 2 * edge, fine), lambda o, *_: (o, 0, 0)),
            scratch_shapes=[
                pltpu.VMEM((nt, 2 * edge, edge), jnp.bfloat16),
                pltpu.VMEM((nt + 1, 2 * edge, edge), jnp.float32),
                pltpu.SMEM((nt + 1,), jnp.int32),
            ],
        ),
        out_shape=jax.ShapeDtypeStruct((offsets, 2 * edge, fine), jnp.bfloat16),
        compiler_params=pltpu.CompilerParams(vmem_limit_bytes=VMEM),
        cost_estimate=pl.CostEstimate(flops=1, bytes_accessed=1, transcendentals=0),
    )(rows, cols, live, core, p0, p1, tiles)


def tied(value, *others):
    return lax.optimization_barrier((value, *others))[0]


def blocks_kernel(plan, choice, core, mine, theirs, *rest):
    panels, (keep, give, acc) = rest[:-3], rest[-3:]
    j, k = pl.program_id(0), pl.program_id(1)
    width = keep.shape[-1]

    @pl.when(k == 0)
    def _():
        acc[...] = jnp.zeros_like(acc)

    for at, offset in enumerate(plan):
        for chunk, options in enumerate(offset):
            for pick, which in options:
                here = (j == at) & (k == chunk)

                @pl.when(here if pick is None else here & (choice[0] == pick))
                def _():
                    panel = panels[which][...]
                    acc[...] += jnp.dot(
                        mine[0], panel, preferred_element_type=jnp.float32
                    ) + jnp.dot(theirs[0], panel, preferred_element_type=jnp.float32)

    @pl.when(k == pl.num_programs(1) - 1)
    def _():
        keep[0] = acc[pl.ds(pl.multiple_of(core[0] * width, width), width), :]
        give[0] = acc[pl.ds(pl.multiple_of((1 - core[0]) * width, width), width), :]


def blocks(offsets, pieces, choice, core, mine, theirs):
    width = theirs.shape[1] // 2
    chunks = theirs.shape[2] // CHUNK
    arrays, specs, plan = [], [], []
    for o in offsets:
        plan.append([])
        for options in pieces[o]:
            plan[-1].append([])
            for pick, array, block in options:
                plan[-1][-1].append((pick, len(arrays)))
                arrays.append(array)
                specs.append(pl.BlockSpec((CHUNK, width), lambda j, k, *_, block=block: (block, 0)))

    def factor(j, k, *_):
        return (sum(jnp.where(j == at, o, 0) for at, o in enumerate(offsets)), 0, k)

    return pl.pallas_call(
        lambda *refs: blocks_kernel(plan, *refs),
        grid_spec=pltpu.PrefetchScalarGridSpec(
            num_scalar_prefetch=2,
            grid=(len(offsets), chunks),
            in_specs=[pl.BlockSpec((1, 2 * width, CHUNK), factor)] * 2 + specs,
            out_specs=[pl.BlockSpec((1, width, width), lambda j, k, *_: (j, 0, 0))] * 2,
            scratch_shapes=[pltpu.VMEM((2 * width, width), jnp.float32)],
        ),
        out_shape=[jax.ShapeDtypeStruct((len(offsets), width, width), jnp.float32)] * 2,
        compiler_params=pltpu.CompilerParams(vmem_limit_bytes=VMEM),
        cost_estimate=pl.CostEstimate(flops=1, bytes_accessed=1, transcendentals=0),
    )(choice, core, mine, theirs, *arrays)


def on_device(prolong, tiles, tile_rows, tile_cols, counts):
    slots = tiles.shape[2]
    offsets = tiles.shape[1]
    half = prolong.shape[0] // 2
    core = lax.axis_index("col")
    sub = lax.axis_index("sub")

    away = [(s, (s - 1) % NSUB) for s in range(NSUB) if s % ROW != 0]
    wrap = [(s, s + ROW - 1) for s in range(NSUB) if s % ROW == 0]
    y = shift(prolong, 4)
    near = lax.ppermute(prolong, "sub", away)

    other = swap(prolong)
    live = jnp.clip(counts[0] - core * slots, 0, slots)
    live = jnp.where(sub + jnp.arange(offsets) < NSUB, live, 0).astype(jnp.int32)
    which = jnp.reshape(core, (1,)).astype(jnp.int32)
    last = jnp.reshape(sub % ROW == ROW - 1, (1,)).astype(jnp.int32)
    mine = weights(tile_rows[0], tile_cols[0], live, which, prolong, other, tiles[0])
    theirs = swap(tied(mine, y))

    def found(wanted, pieces):
        return blocks(wanted, pieces, last, which, mine, theirs)

    def rows_of(keep, give):
        got = swap(give)
        return jnp.where(
            core == 0, jnp.concatenate([keep, got], axis=2), jnp.concatenate([got, keep], axis=2)
        )

    def moved(upper, o):
        return lax.ppermute(upper, "sub", [(s, s + o) for s in range(NSUB - o)])

    whole = lambda v: [[(None, v, 0)], [(None, v, 1)]]
    b = shift(y, -1)
    w = lax.ppermute(y, "sub", wrap)
    first = found((0, 4), {0: whole(prolong), 4: whole(y)})
    b_a, p_b = b[:half], near[half:] + w[half:]
    d_b = shift(p_b, 1)
    d_a = shift(b_a, -1)
    pieces = {3: whole(b), 1: [[(0, near, k), (1, w, k)] for k in range(2)]}
    second = found((1, 3), pieces)
    third = found((2,), {2: [[(None, d_a, 0)], [(None, d_b, 0)]]})
    keep, give = (jnp.concatenate(parts) for parts in zip(first, second, third))
    rows = rows_of(keep, give)
    order = (0, 4, 1, 3, 2)
    uppers = {o: rows[k] for k, o in enumerate(order)}
    lowers = {o: moved(uppers[o], o) for o in order[1:]}
    upper = jnp.stack([uppers[o] for o in range(offsets)])
    lower = jnp.stack([lowers[o].T for o in range(1, offsets)])
    return upper[None], lower[None]


def solution(mesh):
    placed = (
        P("sub", "col"),
        P("sub", None, "col", None, None),
        P("sub", None, "col"),
        P("sub", None, "col"),
        P("sub", None),
    )
    return jax.shard_map(
        on_device,
        mesh=mesh,
        in_specs=placed,
        out_specs=(P("sub", None, "col", None), P("sub", None, None, "col")),
        check_vma=False,
    )
```

```python
import jax
import jax.numpy as jnp
from jax import lax
from jax.experimental import pallas as pl
from jax.experimental.pallas import tpu as pltpu
from jax.sharding import PartitionSpec as P

NSUB = 128
ROW = 4
GROUP = 16
CHUNK = 2048
VMEM = 24 * 2**20


def shift(value, distance):
    route = [((s + distance) % NSUB, s) for s in range(NSUB)]
    return lax.ppermute(value, "sub", route)


def swap(value):
    return lax.ppermute(value, "col", [(0, 1), (1, 0)])


def weights_kernel(rows, cols, live, core, p0, p1, tiles, out, pt, acc, seen):
    o = pl.program_id(0)
    edge = tiles.shape[-1]
    nt = p0.shape[0] // edge

    @pl.when(o == 0)
    def _():
        for t in range(nt):
            seen[t] = 0
        seen[nt] = 0

    for at, half in enumerate((p0, p1)):

        @pl.when((o == 0) & (core[0] == 0))
        def _():
            for t in range(nt):
                pt[t, at * edge : (at + 1) * edge, :] = half[t * edge : (t + 1) * edge, :].T

        @pl.when((o == 0) & (core[0] == 1))
        def _():
            for t in range(nt):
                pt[t, (1 - at) * edge : (2 - at) * edge, :] = half[t * edge : (t + 1) * edge, :].T

    n = live[o]

    def group(g, carry):
        parts = []
        for j in range(GROUP):
            p = g * GROUP + j
            parts.append(
                jnp.dot(pt[rows[o, p]], tiles[0, p], preferred_element_type=jnp.float32)
            )
        for j in range(GROUP):
            p = g * GROUP + j
            c = jnp.where(p < n, cols[o, p], nt)
            fresh = seen[c] != o + 1
            seen[c] = o + 1
            acc[c] = jnp.where(fresh, parts[j], acc[c] + parts[j])
        return carry

    lax.fori_loop(0, (n + GROUP - 1) // GROUP, group, 0)
    for t in range(nt):
        out[0, :, t * edge : (t + 1) * edge] = jnp.where(seen[t] == o + 1, acc[t], 0.0).astype(
            out.dtype
        )


def weights(rows, cols, live, core, p0, p1, tiles):
    offsets, slots, edge, _ = tiles.shape
    fine = p0.shape[0]
    nt = fine // edge
    whole = lambda o, *_: (0, 0)
    return pl.pallas_call(
        weights_kernel,
        grid_spec=pltpu.PrefetchScalarGridSpec(
            num_scalar_prefetch=4,
            grid=(offsets,),
            in_specs=[
                pl.BlockSpec((fine, edge), whole),
                pl.BlockSpec((fine, edge), whole),
                pl.BlockSpec((1, slots, edge, edge), lambda o, *_: (o, 0, 0, 0)),
            ],
            out_specs=pl.BlockSpec((1, 2 * edge, fine), lambda o, *_: (o, 0, 0)),
            scratch_shapes=[
                pltpu.VMEM((nt, 2 * edge, edge), jnp.bfloat16),
                pltpu.VMEM((nt + 1, 2 * edge, edge), jnp.float32),
                pltpu.SMEM((nt + 1,), jnp.int32),
            ],
        ),
        out_shape=jax.ShapeDtypeStruct((offsets, 2 * edge, fine), jnp.bfloat16),
        compiler_params=pltpu.CompilerParams(vmem_limit_bytes=VMEM),
        cost_estimate=pl.CostEstimate(flops=1, bytes_accessed=1, transcendentals=0),
    )(rows, cols, live, core, p0, p1, tiles)


def tied(value, *others):
    return lax.optimization_barrier((value, *others))[0]


def blocks_kernel(plan, choice, core, mine, theirs, *rest):
    panels, (keep, give, acc) = rest[:-3], rest[-3:]
    j, k = pl.program_id(0), pl.program_id(1)
    width = keep.shape[-1]

    @pl.when(k == 0)
    def _():
        acc[...] = jnp.zeros_like(acc)

    for at, offset in enumerate(plan):
        for chunk, options in enumerate(offset):
            for pick, which in options:
                here = (j == at) & (k == chunk)

                @pl.when(here if pick is None else here & (choice[0] == pick))
                def _():
                    panel = panels[which][...]
                    acc[...] += jnp.dot(
                        mine[0], panel, preferred_element_type=jnp.float32
                    ) + jnp.dot(theirs[0], panel, preferred_element_type=jnp.float32)

    @pl.when(k == pl.num_programs(1) - 1)
    def _():
        keep[0] = acc[pl.ds(pl.multiple_of(core[0] * width, width), width), :]
        give[0] = acc[pl.ds(pl.multiple_of((1 - core[0]) * width, width), width), :]


def blocks(offsets, pieces, choice, core, mine, theirs):
    width = theirs.shape[1] // 2
    chunks = theirs.shape[2] // CHUNK
    arrays, specs, plan = [], [], []
    for o in offsets:
        plan.append([])
        for options in pieces[o]:
            plan[-1].append([])
            for pick, array, block in options:
                plan[-1][-1].append((pick, len(arrays)))
                arrays.append(array)
                specs.append(pl.BlockSpec((CHUNK, width), lambda j, k, *_, block=block: (block, 0)))

    def factor(j, k, *_):
        return (sum(jnp.where(j == at, o, 0) for at, o in enumerate(offsets)), 0, k)

    return pl.pallas_call(
        lambda *refs: blocks_kernel(plan, *refs),
        grid_spec=pltpu.PrefetchScalarGridSpec(
            num_scalar_prefetch=2,
            grid=(len(offsets), chunks),
            in_specs=[pl.BlockSpec((1, 2 * width, CHUNK), factor)] * 2 + specs,
            out_specs=[pl.BlockSpec((1, width, width), lambda j, k, *_: (j, 0, 0))] * 2,
            scratch_shapes=[pltpu.VMEM((2 * width, width), jnp.float32)],
        ),
        out_shape=[jax.ShapeDtypeStruct((len(offsets), width, width), jnp.float32)] * 2,
        compiler_params=pltpu.CompilerParams(vmem_limit_bytes=VMEM),
        cost_estimate=pl.CostEstimate(flops=1, bytes_accessed=1, transcendentals=0),
    )(choice, core, mine, theirs, *arrays)


def on_device(prolong, tiles, tile_rows, tile_cols, counts):
    slots = tiles.shape[2]
    offsets = tiles.shape[1]
    half = prolong.shape[0] // 2
    core = lax.axis_index("col")
    sub = lax.axis_index("sub")

    away = [(s, (s - 1) % NSUB) for s in range(NSUB) if s % ROW != 0]
    wrap = [(s, s + ROW - 1) for s in range(NSUB) if s % ROW == 0]
    y = shift(prolong, 4)
    near = lax.ppermute(prolong, "sub", away)

    other = swap(prolong)
    live = jnp.clip(counts[0] - core * slots, 0, slots)
    live = jnp.where(sub + jnp.arange(offsets) < NSUB, live, 0).astype(jnp.int32)
    which = jnp.reshape(core, (1,)).astype(jnp.int32)
    last = jnp.reshape(sub % ROW == ROW - 1, (1,)).astype(jnp.int32)
    mine = weights(tile_rows[0], tile_cols[0], live, which, prolong, other, tiles[0])
    theirs = swap(tied(mine, y))

    def found(wanted, pieces):
        return blocks(wanted, pieces, last, which, mine, theirs)

    def rows_of(keep, give):
        got = swap(give)
        return jnp.where(
            core == 0, jnp.concatenate([keep, got], axis=2), jnp.concatenate([got, keep], axis=2)
        )

    def moved(upper, o):
        return lax.ppermute(upper, "sub", [(s, s + o) for s in range(NSUB - o)])

    whole = lambda v: [[(None, v, 0)], [(None, v, 1)]]
    b_b = shift(prolong[half:], 3)
    b_a = shift(y[:half], -1)
    w = lax.ppermute(y, "sub", wrap)
    first = found((0, 4), {0: whole(prolong), 4: whole(y)})
    d_a = shift(b_a, -1)
    d_b = shift(near[half:] + w[half:], 1)
    pieces = {
        3: [[(None, b_a, 0)], [(None, b_b, 0)]],
        1: [[(0, near, k), (1, w, k)] for k in range(2)],
    }
    second = found((1, 3), pieces)
    third = found((2,), {2: [[(None, d_a, 0)], [(None, d_b, 0)]]})
    keep, give = (jnp.concatenate(parts) for parts in zip(first, second, third))
    rows = rows_of(keep, give)
    order = (0, 4, 1, 3, 2)
    uppers = {o: rows[k] for k, o in enumerate(order)}
    lowers = {o: moved(uppers[o], o) for o in order[1:]}
    upper = jnp.stack([uppers[o] for o in range(offsets)])
    lower = jnp.stack([lowers[o].T for o in range(1, offsets)])
    return upper[None], lower[None]


def solution(mesh):
    placed = (
        P("sub", "col"),
        P("sub", None, "col", None, None),
        P("sub", None, "col"),
        P("sub", None, "col"),
        P("sub", None),
    )
    return jax.shard_map(
        on_device,
        mesh=mesh,
        in_specs=placed,
        out_specs=(P("sub", None, "col", None), P("sub", None, None, "col")),
        check_vma=False,
    )
```
